32 devices in a mesh: ctx: 8 (over z, y), kvh: 4 (over x, core).
Axes of the slice: x: 2, y: 2, z: 4, core: 2. Of those that a mesh axis runs over, the one named last changes fastest.
Arguments:
- queries: bfloat16 [1024, 32, 128], P('ctx', 'kvh'), may hold values from -32 to 32
- new_keys: bfloat16 [1024, 8, 128], P('ctx', 'kvh'), may hold values from -6 to 6
- new_values: bfloat16 [1024, 8, 128], P('ctx', 'kvh'), may hold values from -6 to 6
- cache_keys: bfloat16 [65536, 8, 128], P('ctx', 'kvh'), may hold values from -6 to 6
- cache_values: bfloat16 [65536, 8, 128], P('ctx', 'kvh'), may hold values from -6 to 6
- verticals: int32 [32, 16], P('kvh'), may hold values from 0 to 1023, as said below
- offsets: int32 [32, 96], P('kvh'), may hold values from 0 to 255, as said below
- out_weight: bfloat16 [4096, 4096], P('kvh'), may hold values from -0.09375 to 0.09375
Outputs:
- output: bfloat16 [1024, 4096], P(('ctx', 'kvh'))
The draws below stay inside these ranges and needn't reach their ends.
Inputs may be any that keep to these rules, and one draw needn't show every extreme that they name: `verticals`: 16 distinct cache blocks per head; at most 2 of one head's lie among the 128 blocks of one index of ctx, and exactly 2 do for some index, for every head. 96 distinct offsets per head; the first is 0 and the second is 255.
All inputs are finite; a program needn't handle non-finite values.
Results may differ from the reference program's by a relative error of at most 0.015.
Values may be sent and summed in bfloat16 or wider, within the bound.
A program may use at most 256 MiB of HBM per device.

```python
import math
import jax
import jax.numpy as jnp
from jax import lax

D = 4096
HEADS = 32
KV_HEADS = 8
HD = 128
BLOCK = 64
NV = 16
NS = 96
SPAN = 256
VCAP = 2
C_DEV = 8192
STRETCH = 1024
CACHE = 65536


def draw_queries(key, part):
    key = jax.random.fold_in(key, 3)
    base = jnp.clip(jax.random.normal(key, (STRETCH, HEADS, HD), jnp.float32), -6.0, 6.0)
    return base.astype(jnp.bfloat16)


def draw_new_keys(key, part):
    key = jax.random.fold_in(key, 5)
    base = jnp.clip(jax.random.normal(key, (STRETCH, KV_HEADS, HD), jnp.float32), -6.0, 6.0)
    return base.astype(jnp.bfloat16)


def shuffle_ranges(order_key):
    return jax.random.permutation(order_key, CACHE // C_DEV - 1)


def draw_verticals(key, part):
    key = jax.random.fold_in(key, 11)
    blocks_dev = C_DEV // BLOCK
    ranges = CACHE // C_DEV
    others = ranges - 1
    stride = blocks_dev // VCAP
    hot_key, order_key, jitter_key = jax.random.split(key, 3)
    hot_range = jax.random.randint(hot_key, (HEADS, 1), 0, ranges)
    orders = jax.vmap(shuffle_ranges)(jax.random.split(order_key, HEADS)).astype(jnp.int32)
    position = jnp.arange(NV, dtype=jnp.int32)[None, :]
    remaining = jnp.maximum(position - VCAP, 0)
    chosen = jnp.take_along_axis(orders, jnp.broadcast_to(remaining % others, (HEADS, NV)), axis=1)
    device = jnp.where(position < VCAP, hot_range, (hot_range + 1 + chosen) % ranges)
    slot = jnp.where(position < VCAP, position, remaining // others)
    jitter = jax.random.randint(jitter_key, (HEADS, NV), 0, stride)
    return (device * blocks_dev + slot * stride + jitter).astype(jnp.int32)


def one_offset_row(row_key):
    order = jax.random.permutation(row_key, SPAN - 2)[:NS - 2].astype(jnp.int32) + 1
    first_two = jnp.array([0, SPAN - 1], dtype=jnp.int32)
    return jnp.concatenate([first_two, order])


def draw_offsets(key, part):
    key = jax.random.fold_in(key, 23)
    return jax.vmap(one_offset_row)(jax.random.split(key, HEADS)).astype(jnp.int32)


def steps_of(key, dims, shards, least, largest):
    def one(dim, blocks):
        draws = jax.random.uniform(jax.random.fold_in(jax.random.fold_in(key, 6), dim), (blocks,), jnp.float32, least / len(shards), largest / len(shards))
        return jnp.repeat(jnp.exp(draws), dims[dim] // blocks).reshape((-1,) + (1,) * (len(dims) - dim - 1))

    loudness = one(*shards[0])
    for cut in shards[1:]:
        loudness = loudness * one(*cut)
    return loudness


def gaussian(rng, dims, width, limit, cuts=(), kind=jnp.bfloat16):
    result = jax.random.normal(rng, dims, jnp.float32) * width
    if len(cuts) > 0:
        result = steps_of(rng, dims, cuts, -0.22, 0.18) * result
    return jnp.clip(result, min=-limit, max=limit).astype(kind)


def setup_inputs(seed: int = 0) -> dict:
    key_list = jax.random.split(jax.random.key(seed), 9)
    queries = draw_queries(jax.random.fold_in(key_list[8], 71), 0)
    new_keys = draw_new_keys(jax.random.fold_in(key_list[8], 71), 0)
    new_values = gaussian(key_list[2], (STRETCH, KV_HEADS, HD), 1.0, 6.0, ((0, 8), (1, 4)))
    cache_keys = gaussian(key_list[3], (CACHE, KV_HEADS, HD), 1.0, 6.0, ((0, 8), (1, 4)))
    cache_values = gaussian(key_list[4], (CACHE, KV_HEADS, HD), 1.0, 6.0, ((0, 8), (1, 4)))
    verticals = draw_verticals(jax.random.fold_in(key_list[8], 71), 0)
    offsets = draw_offsets(jax.random.fold_in(key_list[8], 71), 0)
    out_weight = gaussian(key_list[7], (HEADS * HD, D), (HEADS * HD) ** -0.5, 0.09375, ((0, 4),))
    return dict(queries=queries, new_keys=new_keys, new_values=new_values, cache_keys=cache_keys, cache_values=cache_values, verticals=verticals, offsets=offsets, out_weight=out_weight)


lowest_score = -1e+30

def reference(queries, new_keys, new_values, cache_keys, cache_values, verticals, offsets, out_weight):
    stretch_rows, head_count, head_width = queries.shape
    kv_heads = cache_keys.shape[1]
    group_size = head_count // kv_heads
    cache_blocks = cache_keys.shape[0] // BLOCK
    query_blocks = stretch_rows // BLOCK
    scaling = 1.0 / math.sqrt(head_width)
    cache_key_blocks = cache_keys.reshape(cache_blocks, BLOCK, kv_heads, head_width)
    cache_value_blocks = cache_values.reshape(cache_blocks, BLOCK, kv_heads, head_width)
    tail_rows = SPAN * BLOCK
    tail_start = cache_keys.shape[0] - tail_rows
    recent_keys = jnp.concatenate([cache_keys[tail_start:], new_keys], axis=0).reshape(-1, BLOCK, kv_heads, head_width)
    recent_values = jnp.concatenate([cache_values[tail_start:], new_values], axis=0).reshape(-1, BLOCK, kv_heads, head_width)
    block_ids = jnp.arange(query_blocks, dtype=jnp.int32)
    row_pos = jnp.arange(BLOCK, dtype=jnp.int32)[:, None]
    key_pos = jnp.arange(BLOCK, dtype=jnp.int32)[None, :]

    def one_head(pieces):
        head_index, vertical_row, offset_row = pieces
        kv_head = head_index // group_size
        head_rows = jnp.take(queries, head_index, axis=1).reshape(query_blocks, BLOCK, head_width)
        vert_count = vertical_row.shape[0]
        diag_count = offset_row.shape[0]
        vertical_keys = cache_key_blocks[vertical_row, :, kv_head, :]
        vertical_values = cache_value_blocks[vertical_row, :, kv_head, :]
        where_block = SPAN + block_ids[:, None] - offset_row[None, :]
        slash_keys = recent_keys[where_block, :, kv_head, :]
        slash_values = recent_values[where_block, :, kv_head, :]
        key_data = jnp.concatenate([jnp.broadcast_to(vertical_keys[None], (query_blocks, vert_count, BLOCK, head_width)), slash_keys], axis=1)
        value_data = jnp.concatenate([jnp.broadcast_to(vertical_values[None], (query_blocks, vert_count, BLOCK, head_width)), slash_values], axis=1)
        scores = jnp.einsum('brd,bskd->brsk', head_rows.astype(jnp.float32), key_data.astype(jnp.float32)) * scaling
        slash_blocks = cache_blocks + block_ids[:, None, None] - offset_row[None, None, :]
        repeated = jnp.any(vertical_row[None, :, None] == slash_blocks, axis=-1)
        slot_ok = jnp.concatenate([jnp.logical_not(repeated), jnp.ones((query_blocks, diag_count), dtype=jnp.bool_)], axis=1)
        open_slot = jnp.concatenate([jnp.ones((vert_count,), dtype=jnp.bool_), offset_row != 0])
        allowed = slot_ok[:, None, :, None] & (open_slot[None, None, :, None] | (key_pos <= row_pos)[None, :, None, :])
        masked = jnp.where(allowed, scores, lowest_score)
        maximum = lax.optimization_barrier(jnp.max(masked, axis=(2, 3), keepdims=True))
        weights = jnp.where(allowed, jnp.exp(masked - maximum), 0.0)
        totals = lax.optimization_barrier(jnp.sum(weights, axis=(2, 3)))
        rounded = lax.optimization_barrier(weights.astype(jnp.bfloat16)).astype(jnp.float32)
        summed = jnp.einsum('brsk,bskd->brd', rounded, value_data.astype(jnp.float32))
        return (summed / totals[..., None]).reshape(stretch_rows, head_width)
    attended = lax.map(one_head, (jnp.arange(head_count, dtype=jnp.int32), verticals, offsets))
    attended = jnp.transpose(attended, (1, 0, 2)).reshape(stretch_rows, head_count * head_width).astype(jnp.bfloat16)
    return jnp.dot(attended, out_weight, preferred_element_type=jnp.float32).astype(jnp.bfloat16)
```

```python
import functools
import math

import jax
import jax.numpy as jnp
from jax import lax
from jax.experimental import pallas as pl
from jax.experimental.pallas import tpu as pltpu
from jax.sharding import PartitionSpec as P

BLOCK = 64
SPAN = 256
VCAP = 2
GROUP = 8
LOWEST = -1e30
MESH = pl.DeviceIdType.MESH
VMEM_LIMIT = 56 * 1024 * 1024


def lane_fold(x, op):
    parts = [x[:, i * 128 : (i + 1) * 128] for i in range(x.shape[1] // 128)]
    return functools.reduce(op, parts)


def to_row(column):
    return jnp.transpose(jnp.broadcast_to(column, (column.shape[0], 128)))[0:1, :]


def slash_kernel(
    factor, heads, base_ref, off_ref, lo_ref, hi_ref, q_ref, k_ref, v_ref, o_ref, lse_ref, s_ref
):
    kv = pl.program_id(0)
    key_blocks = k_ref.shape[1] // BLOCK
    diagonals = off_ref.shape[1]
    owners = q_ref.shape[0]
    width = GROUP * BLOCK

    def one_pair(it, carry):
        hh = it // owners
        c = it - hh * owners
        h = kv * heads + hh
        spans = [(lo_ref[h, 2 * c + i], hi_ref[h, 2 * c + i]) for i in range(2)]
        counts = [hi - lo for lo, hi in spans]
        groups = lax.div(jnp.maximum(counts[0], counts[1]) + (GROUP - 1), GROUP)

        def gathered(ref, i, t):
            lo, hi = spans[i]
            rows = []
            for g in range(GROUP):
                slot = jnp.clip(jnp.minimum(lo + t * GROUP + g, hi - 1), 0, diagonals - 1)
                j = jnp.clip(base_ref[0] + 2 * c + i - off_ref[h, slot], 0, key_blocks - 1)
                rows.append(ref[0, pl.ds(pl.multiple_of(j * BLOCK, BLOCK), BLOCK), :])
            return jnp.concatenate(rows, axis=0)

        q = [q_ref[c, hh, i * BLOCK : (i + 1) * BLOCK, :] for i in range(2)]

        def first(t, best):
            new = []
            for i in range(2):
                s = lax.dot_general(
                    q[i],
                    gathered(k_ref, i, t),
                    (((1,), (1,)), ((), ())),
                    preferred_element_type=jnp.float32,
                )
                s_ref[i, t] = s
                new.append(jnp.maximum(best[i], lane_fold(s, jnp.maximum)))
            return tuple(new)

        low = jnp.full((BLOCK, 128), LOWEST, jnp.float32)
        best = lax.fori_loop(0, groups, first, (low, low))

        @pl.when(groups > 0)
        def _():
            key = lax.broadcasted_iota(jnp.int32, (BLOCK, width), 1)
            for i in range(2):
                valid = (counts[i] - (groups - 1) * GROUP) * BLOCK
                s_ref[i, groups - 1] = jnp.where(key < valid, s_ref[i, groups - 1], LOWEST)

        top = [jnp.max(b, axis=1, keepdims=True) for b in best]

        def second(t, state):
            new = []
            for i in range(2):
                total, acc = state[i]
                p = jnp.exp2((s_ref[i, t] - top[i]) * factor)
                total = total + lane_fold(p, jnp.add)
                acc = acc + jnp.dot(
                    p.astype(jnp.bfloat16), gathered(v_ref, i, t), preferred_element_type=jnp.float32
                )
                new.append((total, acc))
            return tuple(new)

        zero = jnp.zeros((BLOCK, 128), jnp.float32)
        state = lax.fori_loop(0, groups, second, ((zero, zero), (zero, zero)))
        lse = []
        for i in range(2):
            total = jnp.sum(state[i][0], axis=1, keepdims=True)
            some = total > 0.0
            safe = jnp.where(some, total, 1.0)
            o_ref[c, hh, i * BLOCK : (i + 1) * BLOCK, :] = (state[i][1] / safe).astype(o_ref.dtype)
            lse.append(jnp.where(some, top[i] * factor + jnp.log2(safe), LOWEST))
        lse_ref[c, 0, pl.ds(hh, 1), :] = to_row(jnp.concatenate(lse, axis=0))
        return carry

    lax.fori_loop(0, heads * owners, one_pair, 0)


def slash_attention(base, sorted_offsets, lo, hi, queries, keys, values, factor):
    owners, head_count, rows, hd = queries.shape
    kv_heads, key_rows, _ = keys.shape
    heads = head_count // kv_heads
    most = -(-sorted_offsets.shape[1] // GROUP)
    elements = head_count * rows * owners * 48 * BLOCK
    return pl.pallas_call(
        functools.partial(slash_kernel, factor, heads),
        grid_spec=pltpu.PrefetchScalarGridSpec(
            num_scalar_prefetch=4,
            grid=(kv_heads,),
            in_specs=[
                pl.BlockSpec((owners, heads, rows, hd), lambda g, *_: (0, g, 0, 0)),
                pl.BlockSpec((1, key_rows, hd), lambda g, *_: (g, 0, 0)),
                pl.BlockSpec((1, key_rows, hd), lambda g, *_: (g, 0, 0)),
            ],
            out_specs=[
                pl.BlockSpec((owners, heads, rows, hd), lambda g, *_: (0, g, 0, 0)),
                pl.BlockSpec((owners, 1, heads, rows), lambda g, *_: (0, g, 0, 0)),
            ],
            scratch_shapes=[pltpu.VMEM((2, most, BLOCK, GROUP * BLOCK), jnp.float32)],
        ),
        out_shape=[
            jax.ShapeDtypeStruct(queries.shape, jnp.bfloat16),
            jax.ShapeDtypeStruct((owners, kv_heads, heads, rows), jnp.float32),
        ],
        compiler_params=pltpu.CompilerParams(vmem_limit_bytes=VMEM_LIMIT),
        cost_estimate=pl.CostEstimate(
            flops=4 * elements * hd, bytes_accessed=12 * 2**20, transcendentals=elements
        ),
    )(base, sorted_offsets, lo, hi, queries, keys, values)


def local_kernel(factor, me_ref, q_ref, kv_ref, vv_ref, kn_ref, vn_ref, bias_ref, o_ref, lse_ref):
    rows, hd = q_ref.shape[1:]
    blocks = rows // BLOCK

    def flat(ref):
        return ref[...].reshape(-1, hd)

    def scores(keys, kind):
        s = lax.dot_general(
            q_ref[0], keys, (((1,), (1,)), ((), ())), preferred_element_type=jnp.float32
        )
        bias = bias_ref[0, kind]
        parts = [s[i * BLOCK : (i + 1) * BLOCK] + bias[i : i + 1] for i in range(blocks)]
        return jnp.concatenate(parts, axis=0)

    s_vert = scores(flat(kv_ref), 0)
    s_new = scores(flat(kn_ref), 1)
    key = lax.broadcasted_iota(jnp.int32, s_new.shape, 1)
    row = lax.broadcasted_iota(jnp.int32, s_new.shape, 0) + me_ref[0] * rows
    s_new = jnp.where(key <= row, s_new, LOWEST)
    top = jnp.maximum(
        jnp.max(lane_fold(s_vert, jnp.maximum), axis=1, keepdims=True),
        jnp.max(lane_fold(s_new, jnp.maximum), axis=1, keepdims=True),
    )
    p_vert = jnp.exp2((s_vert - top) * factor)
    p_new = jnp.exp2((s_new - top) * factor)
    total = jnp.sum(lane_fold(p_vert, jnp.add) + lane_fold(p_new, jnp.add), axis=1, keepdims=True)
    acc = jnp.dot(
        p_vert.astype(jnp.bfloat16), flat(vv_ref), preferred_element_type=jnp.float32
    ) + jnp.dot(p_new.astype(jnp.bfloat16), flat(vn_ref), preferred_element_type=jnp.float32)
    o_ref[0] = acc / total
    lse_ref[0] = to_row(top * factor + jnp.log2(total))


def local_attention(me, queries, gathered, bias, kv_heads, factor):
    head_count, rows, hd = queries.shape
    owners = gathered.shape[0]
    blocks = rows // BLOCK
    group = head_count // kv_heads
    piece = (owners, 2, BLOCK, hd)
    return pl.pallas_call(
        functools.partial(local_kernel, factor),
        grid_spec=pltpu.PrefetchScalarGridSpec(
            num_scalar_prefetch=1,
            grid=(head_count,),
            in_specs=[
                pl.BlockSpec((1, rows, hd), lambda h, *_: (h, 0, 0)),
                pl.BlockSpec(piece, lambda h, *_: (0, h, 0, 0)),
                pl.BlockSpec(piece, lambda h, *_: (0, head_count + h, 0, 0)),
                pl.BlockSpec(piece, lambda h, *_: (0, 2 * head_count + h // group, 0, 0)),
                pl.BlockSpec(piece, lambda h, *_: (0, 2 * head_count + kv_heads + h // group, 0, 0)),
                pl.BlockSpec((1, 2, blocks, bias.shape[-1]), lambda h, *_: (h, 0, 0, 0)),
            ],
            out_specs=[
                pl.BlockSpec((1, rows, hd), lambda h, *_: (h, 0, 0)),
                pl.BlockSpec((1, 1, rows), lambda h, *_: (h, 0, 0)),
            ],
        ),
        out_shape=[
            jax.ShapeDtypeStruct(queries.shape, jnp.float32),
            jax.ShapeDtypeStruct((head_count, 1, rows), jnp.float32),
        ],
        compiler_params=pltpu.CompilerParams(vmem_limit_bytes=VMEM_LIMIT),
        cost_estimate=pl.CostEstimate(
            flops=4 * head_count * rows * hd * 2 * bias.shape[-1],
            bytes_accessed=6 * 2**20,
            transcendentals=head_count * rows * 2 * bias.shape[-1],
        ),
    )(me, queries, gathered, gathered, gathered, gathered, bias)


def return_kernel(holders, o_ref, l_ref, part_ref, plse_ref, o_send, l_send, o_recv, l_recv, o_own, l_own):
    size = lax.axis_size("ctx")
    me = lax.axis_index("ctx")
    kvh = lax.axis_index("kvh")
    first = size - holders
    barrier = pltpu.get_barrier_semaphore()
    for r in range(holders):

        @pl.when(me != first + r)
        def _():
            pl.semaphore_signal(barrier, inc=1, device_id=(first + r, kvh), device_id_type=MESH)

    def copies(r, step):
        to = lax.rem(me + step, size)
        pairs = ((o_ref, part_ref, o_send, o_recv), (l_ref, plse_ref, l_send, l_recv))
        return [
            pltpu.make_async_remote_copy(
                src_ref=src.at[to],
                dst_ref=dst.at[r],
                send_sem=send.at[step - 1],
                recv_sem=recv.at[r],
                device_id=(to, kvh),
                device_id_type=MESH,
            )
            for src, dst, send, recv in pairs
        ]

    for r in range(holders):

        @pl.when(me == first + r)
        def _():
            pl.semaphore_wait(barrier, size - 1)
            for step in range(1, size):
                for copy in copies(r, step):
                    copy.start()
            own = [
                pltpu.make_async_copy(o_ref.at[me], part_ref.at[r], o_own),
                pltpu.make_async_copy(l_ref.at[me], plse_ref.at[r], l_own),
            ]
            for copy in own:
                copy.start()
            for copy in own:
                copy.wait()
            for step in range(1, size):
                for copy in copies(r, step):
                    copy.wait_send()

    for r in range(holders):

        @pl.when(me != first + r)
        def _():
            for copy in copies(r, 1):
                copy.wait_recv()


def return_parts(o, lse, holders):
    size = o.shape[0]
    return pl.pallas_call(
        functools.partial(return_kernel, holders),
        out_shape=[
            jax.ShapeDtypeStruct((holders,) + o.shape[1:], o.dtype),
            jax.ShapeDtypeStruct((holders,) + lse.shape[1:], lse.dtype),
        ],
        in_specs=[pl.BlockSpec(memory_space=pl.ANY)] * 2,
        out_specs=[pl.BlockSpec(memory_space=pl.ANY)] * 2,
        scratch_shapes=[
            pltpu.SemaphoreType.DMA((size - 1,)),
            pltpu.SemaphoreType.DMA((size - 1,)),
            pltpu.SemaphoreType.DMA((holders,)),
            pltpu.SemaphoreType.DMA((holders,)),
            pltpu.SemaphoreType.DMA,
            pltpu.SemaphoreType.DMA,
        ],
        compiler_params=pltpu.CompilerParams(collective_id=0, has_side_effects=True),
    )(o, lse)


def slots_of(verticals, lower_block, blocks_dev):
    inside = (verticals >= lower_block) & (verticals < lower_block + blocks_dev)
    counts = inside.astype(jnp.int32)
    slot_rank = jnp.cumsum(counts, axis=1) - counts
    slot_ids = jnp.arange(VCAP, dtype=jnp.int32)
    onehot = inside[:, None, :] & (slot_rank[:, None, :] == slot_ids[None, :, None])
    filled = jnp.any(onehot, axis=2)
    block = jnp.sum(jnp.where(onehot, verticals[:, None, :], 0), axis=2)
    return jnp.where(filled, block, -1)


def shards(queries, new_keys, new_values, cache_keys, cache_values, verticals, offsets, out_weight):
    own_rows, head_count, hd = queries.shape
    kv_heads = cache_keys.shape[1]
    size = lax.axis_size("ctx")
    me = lax.axis_index("ctx")
    cache_rows = cache_keys.shape[0]
    blocks_dev = cache_rows // BLOCK
    cache_blocks = blocks_dev * size
    own_blocks = own_rows // BLOCK
    holders = SPAN // blocks_dev
    group = head_count // kv_heads
    factor = math.log2(math.e) / math.sqrt(hd)

    q_own = jnp.transpose(queries, (1, 0, 2))
    q_all = lax.all_gather(q_own, "ctx", axis=0, tiled=False)

    keys = jnp.transpose(cache_keys, (1, 0, 2))
    values = jnp.transpose(cache_values, (1, 0, 2))
    mine = slots_of(verticals, me * blocks_dev, blocks_dev)
    local_block = jnp.where(mine >= 0, mine - me * blocks_dev, 0)
    kv_of = (jnp.arange(head_count, dtype=jnp.int32) // group)[:, None]
    flat_block = (kv_of * blocks_dev + local_block).reshape(-1)
    slot_keys = keys.reshape(-1, BLOCK, hd)[flat_block]
    slot_values = values.reshape(-1, BLOCK, hd)[flat_block]
    fresh_keys = jnp.transpose(new_keys, (1, 0, 2)).reshape(-1, BLOCK, hd)
    fresh_values = jnp.transpose(new_values, (1, 0, 2)).reshape(-1, BLOCK, hd)
    packed = jnp.concatenate([slot_keys, slot_values, fresh_keys, fresh_values], axis=0)
    gathered = lax.all_gather(packed, "ctx", axis=0, tiled=False)

    rank = jnp.sum((offsets[:, :, None] > offsets[:, None, :]).astype(jnp.int32), axis=2)
    places = jnp.arange(offsets.shape[1], dtype=jnp.int32)
    sorted_offsets = jnp.sum(
        jnp.where(rank[:, :, None] == places[None, None, :], offsets[:, :, None], 0), axis=1
    )
    holder = me - (size - holders)
    base = SPAN - holder * blocks_dev
    block_ids = jnp.arange(size * own_blocks, dtype=jnp.int32)
    highest = (base + block_ids)[None, :, None]
    hi = jnp.sum((offsets[:, None, :] <= highest).astype(jnp.int32), axis=2)
    lo = jnp.sum((offsets[:, None, :] <= highest - blocks_dev).astype(jnp.int32), axis=2)
    is_holder = holder >= 0
    lo = jnp.where(is_holder, lo, 0)
    hi = jnp.where(is_holder, hi, 0)
    slash_o, slash_lse = slash_attention(
        base.reshape(1), sorted_offsets, lo, hi, q_all, keys, values, factor
    )
    part_o, part_lse = return_parts(slash_o, slash_lse, holders)

    own_ids = me * own_blocks + jnp.arange(own_blocks, dtype=jnp.int32)
    slots = jnp.stack([slots_of(verticals, c * blocks_dev, blocks_dev) for c in range(size)], axis=1)
    slots = slots.reshape(head_count, size * VCAP)
    slash_blocks = cache_blocks + own_ids[None, :, None] - offsets[:, None, :]
    repeated = jnp.any(slots[:, None, :, None] == slash_blocks[:, :, None, :], axis=-1)
    vert_ok = (slots[:, None, :] >= 0) & jnp.logical_not(repeated)
    new_ids = cache_blocks + jnp.arange(size * own_blocks, dtype=jnp.int32)
    new_ok = jnp.any(new_ids[None, None, :, None] == slash_blocks[:, :, None, :], axis=-1)
    bias = jnp.where(jnp.stack([vert_ok, new_ok], axis=1), 0.0, LOWEST).astype(jnp.float32)
    bias = jnp.repeat(bias, BLOCK, axis=-1)
    own_o, own_lse = local_attention(me.reshape(1), q_own, gathered, bias, kv_heads, factor)

    own_lse = own_lse.reshape(head_count, own_rows)
    part_lse = part_lse.reshape(holders, head_count, own_rows)
    top = jnp.maximum(own_lse, jnp.max(part_lse, axis=0))
    own_share = jnp.exp2(own_lse - top)
    part_share = jnp.exp2(part_lse - top[None])
    whole = own_share + jnp.sum(part_share, axis=0)
    mixed = own_o * (own_share / whole)[..., None] + jnp.sum(
        part_o.astype(jnp.float32) * (part_share / whole[None])[..., None], axis=0
    )
    attended = jnp.transpose(mixed.astype(jnp.bfloat16), (1, 0, 2)).reshape(own_rows, head_count * hd)
    return lax.psum_scatter(
        jnp.dot(attended, out_weight, preferred_element_type=jnp.float32).astype(jnp.bfloat16),
        "kvh",
        scatter_dimension=0,
        tiled=True,
    )


def solution(mesh):
    return jax.shard_map(
        shards,
        mesh=mesh,
        in_specs=(
            P("ctx", "kvh", None),
            P("ctx", "kvh", None),
            P("ctx", "kvh", None),
            P("ctx", "kvh", None),
            P("ctx", "kvh", None),
            P("kvh", None),
            P("kvh", None),
            P("kvh", None),
        ),
        out_specs=P(("ctx", "kvh"), None),
        check_vma=False,
    )
```

```python
import functools
import math

import jax
import jax.numpy as jnp
from jax import lax
from jax.experimental import pallas as pl
from jax.experimental.pallas import tpu as pltpu
from jax.sharding import PartitionSpec as P

BLOCK = 64
SPAN = 256
VCAP = 2
GROUP = 12
BUNDLE = 4
LOWEST = -1e30
MESH = pl.DeviceIdType.MESH
VMEM_LIMIT = 56 * 1024 * 1024


def lane_fold(x, op):
    parts = [x[:, i * 128 : (i + 1) * 128] for i in range(x.shape[1] // 128)]
    return functools.reduce(op, parts)


def to_row(column):
    return jnp.transpose(jnp.broadcast_to(column, (column.shape[0], 128)))[0:1, :]


def slash_kernel(
    factor, heads, length, list_ref, count_ref, q_ref, k_ref, v_ref, o_ref, lse_ref, s_ref
):
    kv = pl.program_id(0)
    owners = q_ref.shape[0]
    width = GROUP * BLOCK
    bundle = min(BUNDLE, heads)
    chains = [(a, i) for a in range(bundle) for i in range(2)]

    def one_bundle(it, carry):
        first_head = (it // owners) * bundle
        c = lax.rem(it, owners)
        hh = [first_head + a for a, _ in chains]
        block = [2 * c + i for _, i in chains]
        pair = [(kv * heads + h) * (2 * owners) + b for h, b in zip(hh, block)]
        counts = [count_ref[p] for p in pair]
        most = functools.reduce(jnp.maximum, counts)
        groups = lax.div(most + (GROUP - 1), GROUP)

        def gathered(ref, n, t):
            at = pair[n] * length + t * GROUP
            rows = [
                ref[0, pl.ds(pl.multiple_of(list_ref[at + g], BLOCK), BLOCK), :] for g in range(GROUP)
            ]
            return jnp.concatenate(rows, axis=0)

        def first(t, best):
            new = []
            for n, (_, i) in enumerate(chains):
                s = lax.dot_general(
                    q_ref[c, hh[n], i * BLOCK : (i + 1) * BLOCK, :],
                    gathered(k_ref, n, t),
                    (((1,), (1,)), ((), ())),
                    preferred_element_type=jnp.float32,
                )
                s_ref[n, t] = s
                new.append(jnp.maximum(best[n], lane_fold(s, jnp.maximum)))
            return tuple(new)

        low = jnp.full((BLOCK, 128), LOWEST, jnp.float32)
        best = lax.fori_loop(0, groups, first, (low,) * len(chains))

        key = lax.broadcasted_iota(jnp.int32, (BLOCK, width), 1)
        for n in range(len(chains)):

            def hide(t, carry, n=n):
                s_ref[n, t] = jnp.where(key < (counts[n] - t * GROUP) * BLOCK, s_ref[n, t], LOWEST)
                return carry

            lax.fori_loop(lax.div(counts[n], GROUP), groups, hide, 0)

        top = [jnp.max(b, axis=1, keepdims=True) for b in best]

        def second(t, state):
            new = []
            for n in range(len(chains)):
                total, acc = state[n]
                p = jnp.exp2((s_ref[n, t] - top[n]) * factor)
                total = total + lane_fold(p, jnp.add)
                acc = acc + jnp.dot(
                    p.astype(jnp.bfloat16), gathered(v_ref, n, t), preferred_element_type=jnp.float32
                )
                new.append((total, acc))
            return tuple(new)

        zero = jnp.zeros((BLOCK, 128), jnp.float32)
        state = lax.fori_loop(0, groups, second, ((zero, zero),) * len(chains))
        lse = []
        for n, (_, i) in enumerate(chains):
            total = jnp.sum(state[n][0], axis=1, keepdims=True)
            some = total > 0.0
            safe = jnp.where(some, total, 1.0)
            part = (state[n][1] / safe).astype(o_ref.dtype)
            o_ref[c, hh[n], i * BLOCK : (i + 1) * BLOCK, :] = part
            lse.append(jnp.where(some, top[n] * factor + jnp.log2(safe), LOWEST))
        for a in range(bundle):
            row = to_row(jnp.concatenate(lse[2 * a : 2 * a + 2], axis=0))
            lse_ref[c, 0, pl.ds(first_head + a, 1), :] = row
        return carry

    lax.fori_loop(0, heads // bundle * owners, one_bundle, 0)


def slash_attention(lists, counts, queries, keys, values, factor):
    owners, head_count, rows, hd = queries.shape
    kv_heads, key_rows, _ = keys.shape
    heads = head_count // kv_heads
    length = lists.shape[-1]
    most = length // GROUP
    elements = head_count * rows * owners * 48 * BLOCK
    return pl.pallas_call(
        functools.partial(slash_kernel, factor, heads, length),
        grid_spec=pltpu.PrefetchScalarGridSpec(
            num_scalar_prefetch=2,
            grid=(kv_heads,),
            in_specs=[
                pl.BlockSpec((owners, heads, rows, hd), lambda g, *_: (0, g, 0, 0)),
                pl.BlockSpec((1, key_rows, hd), lambda g, *_: (g, 0, 0)),
                pl.BlockSpec((1, key_rows, hd), lambda g, *_: (g, 0, 0)),
            ],
            out_specs=[
                pl.BlockSpec((owners, heads, rows, hd), lambda g, *_: (0, g, 0, 0)),
                pl.BlockSpec((owners, 1, heads, rows), lambda g, *_: (0, g, 0, 0)),
            ],
            scratch_shapes=[pltpu.VMEM((2 * min(BUNDLE, heads), most, BLOCK, GROUP * BLOCK), jnp.float32)],
        ),
        out_shape=[
            jax.ShapeDtypeStruct(queries.shape, jnp.bfloat16),
            jax.ShapeDtypeStruct((owners, kv_heads, heads, rows), jnp.float32),
        ],
        compiler_params=pltpu.CompilerParams(vmem_limit_bytes=VMEM_LIMIT),
        cost_estimate=pl.CostEstimate(
            flops=4 * elements * hd, bytes_accessed=12 * 2**20, transcendentals=elements
        ),
    )(lists.reshape(-1), counts.reshape(-1), queries, keys, values)


def local_kernel(factor, me_ref, q_ref, kv_ref, vv_ref, kn_ref, vn_ref, bias_ref, o_ref, lse_ref):
    rows, hd = q_ref.shape[1:]
    blocks = rows // BLOCK

    def flat(ref):
        return ref[...].reshape(-1, hd)

    def scores(keys, kind):
        s = lax.dot_general(
            q_ref[0], keys, (((1,), (1,)), ((), ())), preferred_element_type=jnp.float32
        )
        bias = bias_ref[0, kind]
        parts = [s[i * BLOCK : (i + 1) * BLOCK] + bias[i : i + 1] for i in range(blocks)]
        return jnp.concatenate(parts, axis=0)

    s_vert = scores(flat(kv_ref), 0)
    s_new = scores(flat(kn_ref), 1)
    key = lax.broadcasted_iota(jnp.int32, s_new.shape, 1)
    row = lax.broadcasted_iota(jnp.int32, s_new.shape, 0) + me_ref[0] * rows
    s_new = jnp.where(key <= row, s_new, LOWEST)
    top = jnp.maximum(
        jnp.max(lane_fold(s_vert, jnp.maximum), axis=1, keepdims=True),
        jnp.max(lane_fold(s_new, jnp.maximum), axis=1, keepdims=True),
    )
    p_vert = jnp.exp2((s_vert - top) * factor)
    p_new = jnp.exp2((s_new - top) * factor)
    total = jnp.sum(lane_fold(p_vert, jnp.add) + lane_fold(p_new, jnp.add), axis=1, keepdims=True)
    acc = jnp.dot(
        p_vert.astype(jnp.bfloat16), flat(vv_ref), preferred_element_type=jnp.float32
    ) + jnp.dot(p_new.astype(jnp.bfloat16), flat(vn_ref), preferred_element_type=jnp.float32)
    o_ref[0] = acc / total
    lse_ref[0] = to_row(top * factor + jnp.log2(total))


def local_attention(me, queries, gathered, bias, kv_heads, factor):
    head_count, rows, hd = queries.shape
    owners = gathered.shape[0]
    blocks = rows // BLOCK
    group = head_count // kv_heads
    piece = (owners, 2, BLOCK, hd)
    return pl.pallas_call(
        functools.partial(local_kernel, factor),
        grid_spec=pltpu.PrefetchScalarGridSpec(
            num_scalar_prefetch=1,
            grid=(head_count,),
            in_specs=[
                pl.BlockSpec((1, rows, hd), lambda h, *_: (h, 0, 0)),
                pl.BlockSpec(piece, lambda h, *_: (0, h, 0, 0)),
                pl.BlockSpec(piece, lambda h, *_: (0, head_count + h, 0, 0)),
                pl.BlockSpec(piece, lambda h, *_: (0, 2 * head_count + h // group, 0, 0)),
                pl.BlockSpec(piece, lambda h, *_: (0, 2 * head_count + kv_heads + h // group, 0, 0)),
                pl.BlockSpec((1, 2, blocks, bias.shape[-1]), lambda h, *_: (h, 0, 0, 0)),
            ],
            out_specs=[
                pl.BlockSpec((1, rows, hd), lambda h, *_: (h, 0, 0)),
                pl.BlockSpec((1, 1, rows), lambda h, *_: (h, 0, 0)),
            ],
        ),
        out_shape=[
            jax.ShapeDtypeStruct(queries.shape, jnp.float32),
            jax.ShapeDtypeStruct((head_count, 1, rows), jnp.float32),
        ],
        compiler_params=pltpu.CompilerParams(vmem_limit_bytes=VMEM_LIMIT),
        cost_estimate=pl.CostEstimate(
            flops=4 * head_count * rows * hd * 2 * bias.shape[-1],
            bytes_accessed=6 * 2**20,
            transcendentals=head_count * rows * 2 * bias.shape[-1],
        ),
    )(me, queries, gathered, gathered, gathered, gathered, bias)


def return_kernel(holders, o_ref, l_ref, part_ref, plse_ref, o_send, l_send, o_recv, l_recv, o_own, l_own):
    size = lax.axis_size("ctx")
    me = lax.axis_index("ctx")
    kvh = lax.axis_index("kvh")
    first = size - holders
    barrier = pltpu.get_barrier_semaphore()
    for r in range(holders):

        @pl.when(me != first + r)
        def _():
            pl.semaphore_signal(barrier, inc=1, device_id=(first + r, kvh), device_id_type=MESH)

    def copies(r, step):
        to = lax.rem(me + step, size)
        pairs = ((o_ref, part_ref, o_send, o_recv), (l_ref, plse_ref, l_send, l_recv))
        return [
            pltpu.make_async_remote_copy(
                src_ref=src.at[to],
                dst_ref=dst.at[r],
                send_sem=send.at[step - 1],
                recv_sem=recv.at[r],
                device_id=(to, kvh),
                device_id_type=MESH,
            )
            for src, dst, send, recv in pairs
        ]

    for r in range(holders):

        @pl.when(me == first + r)
        def _():
            pl.semaphore_wait(barrier, size - 1)
            for step in range(1, size):
                for copy in copies(r, step):
                    copy.start()
            own = [
                pltpu.make_async_copy(o_ref.at[me], part_ref.at[r], o_own),
                pltpu.make_async_copy(l_ref.at[me], plse_ref.at[r], l_own),
            ]
            for copy in own:
                copy.start()
            for copy in own:
                copy.wait()
            for step in range(1, size):
                for copy in copies(r, step):
                    copy.wait_send()

    for r in range(holders):

        @pl.when(me != first + r)
        def _():
            for copy in copies(r, 1):
                copy.wait_recv()


def return_parts(o, lse, holders):
    size = o.shape[0]
    return pl.pallas_call(
        functools.partial(return_kernel, holders),
        out_shape=[
            jax.ShapeDtypeStruct((holders,) + o.shape[1:], o.dtype),
            jax.ShapeDtypeStruct((holders,) + lse.shape[1:], lse.dtype),
        ],
        in_specs=[pl.BlockSpec(memory_space=pl.ANY)] * 2,
        out_specs=[pl.BlockSpec(memory_space=pl.ANY)] * 2,
        scratch_shapes=[
            pltpu.SemaphoreType.DMA((size - 1,)),
            pltpu.SemaphoreType.DMA((size - 1,)),
            pltpu.SemaphoreType.DMA((holders,)),
            pltpu.SemaphoreType.DMA((holders,)),
            pltpu.SemaphoreType.DMA,
            pltpu.SemaphoreType.DMA,
        ],
        compiler_params=pltpu.CompilerParams(collective_id=0, has_side_effects=True),
    )(o, lse)


def spread_kernel(y_ref, got_ref, send, recv):
    size = lax.axis_size("kvh")
    me = lax.axis_index("kvh")
    ctx = lax.axis_index("ctx")
    barrier = pltpu.get_barrier_semaphore()
    for step in range(1, size):
        to = lax.rem(me + step, size)
        pl.semaphore_signal(barrier, inc=1, device_id=(ctx, to), device_id_type=MESH)
    pl.semaphore_wait(barrier, size - 1)
    copies = []
    for step in range(1, size):
        to = lax.rem(me + step, size)
        copies.append(
            pltpu.make_async_remote_copy(
                src_ref=y_ref.at[to],
                dst_ref=got_ref.at[step - 1],
                send_sem=send.at[step - 1],
                recv_sem=recv.at[step - 1],
                device_id=(ctx, to),
                device_id_type=MESH,
            )
        )
    for copy in copies:
        copy.start()
    for copy in copies:
        copy.wait()


def sum_over_kvh(y):
    size = lax.axis_size("kvh")
    y = y.reshape(size, y.shape[0] // size, y.shape[1])
    got = pl.pallas_call(
        spread_kernel,
        out_shape=jax.ShapeDtypeStruct((size - 1,) + y.shape[1:], y.dtype),
        in_specs=[pl.BlockSpec(memory_space=pl.ANY)],
        out_specs=pl.BlockSpec(memory_space=pl.ANY),
        scratch_shapes=[
            pltpu.SemaphoreType.DMA((size - 1,)),
            pltpu.SemaphoreType.DMA((size - 1,)),
        ],
        compiler_params=pltpu.CompilerParams(collective_id=1, has_side_effects=True),
    )(y)
    own = lax.dynamic_index_in_dim(y, lax.axis_index("kvh"), axis=0, keepdims=False)
    total = own.astype(jnp.float32) + jnp.sum(got.astype(jnp.float32), axis=0)
    return total.astype(y.dtype)


def block_lists(offsets, block_ids, base, blocks_dev):
    diagonals = offsets.shape[1]
    length = -(-diagonals // GROUP) * GROUP
    rank = jnp.sum((offsets[:, :, None] > offsets[:, None, :]).astype(jnp.int32), axis=2)
    found = base + block_ids[None, :, None] - offsets[:, None, :]
    inside = (found >= 0) & (found < blocks_dev)
    counts = jnp.sum(inside.astype(jnp.int32), axis=2)
    below = jnp.sum((found >= blocks_dev).astype(jnp.int32), axis=2)
    place = jnp.arange(length, dtype=jnp.int32)
    place = below[:, :, None] + jnp.minimum(place[None, None, :], counts[:, :, None] - 1)
    chosen = inside[:, :, None, :] & (rank[:, None, None, :] == place[:, :, :, None])
    lists = jnp.sum(jnp.where(chosen, found[:, :, None, :] * BLOCK, 0), axis=3)
    return lists, counts


def slots_of(verticals, lower_block, blocks_dev):
    inside = (verticals >= lower_block) & (verticals < lower_block + blocks_dev)
    counts = inside.astype(jnp.int32)
    slot_rank = jnp.cumsum(counts, axis=1) - counts
    slot_ids = jnp.arange(VCAP, dtype=jnp.int32)
    onehot = inside[:, None, :] & (slot_rank[:, None, :] == slot_ids[None, :, None])
    filled = jnp.any(onehot, axis=2)
    block = jnp.sum(jnp.where(onehot, verticals[:, None, :], 0), axis=2)
    return jnp.where(filled, block, -1)


def shards(queries, new_keys, new_values, cache_keys, cache_values, verticals, offsets, out_weight):
    own_rows, head_count, hd = queries.shape
    kv_heads = cache_keys.shape[1]
    size = lax.axis_size("ctx")
    me = lax.axis_index("ctx")
    cache_rows = cache_keys.shape[0]
    blocks_dev = cache_rows // BLOCK
    cache_blocks = blocks_dev * size
    own_blocks = own_rows // BLOCK
    holders = SPAN // blocks_dev
    group = head_count // kv_heads
    factor = math.log2(math.e) / math.sqrt(hd)

    q_own = jnp.transpose(queries, (1, 0, 2))
    q_all = lax.all_gather(q_own, "ctx", axis=0, tiled=False)

    keys = jnp.transpose(cache_keys, (1, 0, 2))
    values = jnp.transpose(cache_values, (1, 0, 2))
    mine = slots_of(verticals, me * blocks_dev, blocks_dev)
    local_block = jnp.where(mine >= 0, mine - me * blocks_dev, 0)
    kv_of = (jnp.arange(head_count, dtype=jnp.int32) // group)[:, None]
    flat_block = (kv_of * blocks_dev + local_block).reshape(-1)
    slot_keys = keys.reshape(-1, BLOCK, hd)[flat_block]
    slot_values = values.reshape(-1, BLOCK, hd)[flat_block]
    fresh_keys = jnp.transpose(new_keys, (1, 0, 2)).reshape(-1, BLOCK, hd)
    fresh_values = jnp.transpose(new_values, (1, 0, 2)).reshape(-1, BLOCK, hd)
    packed = jnp.concatenate([slot_keys, slot_values, fresh_keys, fresh_values], axis=0)
    gathered = lax.all_gather(packed, "ctx", axis=0, tiled=False)

    holder = me - (size - holders)
    block_ids = jnp.arange(size * own_blocks, dtype=jnp.int32)
    lists, counts = block_lists(offsets, block_ids, SPAN - holder * blocks_dev, blocks_dev)
    counts = jnp.where(holder >= 0, counts, 0)
    slash_o, slash_lse = slash_attention(lists, counts, q_all, keys, values, factor)
    part_o, part_lse = return_parts(slash_o, slash_lse, holders)

    own_ids = me * own_blocks + jnp.arange(own_blocks, dtype=jnp.int32)
    slots = jnp.stack([slots_of(verticals, c * blocks_dev, blocks_dev) for c in range(size)], axis=1)
    slots = slots.reshape(head_count, size * VCAP)
    slash_blocks = cache_blocks + own_ids[None, :, None] - offsets[:, None, :]
    repeated = jnp.any(slots[:, None, :, None] == slash_blocks[:, :, None, :], axis=-1)
    vert_ok = (slots[:, None, :] >= 0) & jnp.logical_not(repeated)
    new_ids = cache_blocks + jnp.arange(size * own_blocks, dtype=jnp.int32)
    new_ok = jnp.any(new_ids[None, None, :, None] == slash_blocks[:, :, None, :], axis=-1)
    bias = jnp.where(jnp.stack([vert_ok, new_ok], axis=1), 0.0, LOWEST).astype(jnp.float32)
    bias = jnp.repeat(bias, BLOCK, axis=-1)
    own_o, own_lse = local_attention(me.reshape(1), q_own, gathered, bias, kv_heads, factor)

    own_lse = own_lse.reshape(head_count, own_rows)
    part_lse = part_lse.reshape(holders, head_count, own_rows)
    top = jnp.maximum(own_lse, jnp.max(part_lse, axis=0))
    own_share = jnp.exp2(own_lse - top)
    part_share = jnp.exp2(part_lse - top[None])
    whole = own_share + jnp.sum(part_share, axis=0)
    mixed = own_o * (own_share / whole)[..., None] + jnp.sum(
        part_o.astype(jnp.float32) * (part_share / whole[None])[..., None], axis=0
    )
    attended = jnp.transpose(mixed.astype(jnp.bfloat16), (1, 0, 2)).reshape(own_rows, head_count * hd)
    return sum_over_kvh(
        jnp.dot(attended, out_weight, preferred_element_type=jnp.float32).astype(jnp.bfloat16)
    )


def solution(mesh):
    return jax.shard_map(
        shards,
        mesh=mesh,
        in_specs=(
            P("ctx", "kvh", None),
            P("ctx", "kvh", None),
            P("ctx", "kvh", None),
            P("ctx", "kvh", None),
            P("ctx", "kvh", None),
            P("kvh", None),
            P("kvh", None),
            P("kvh", None),
        ),
        out_specs=P(("ctx", "kvh"), None),
        check_vma=False,
    )
```

```python
import functools
import math

import jax
import jax.numpy as jnp
from jax import lax
from jax.experimental import pallas as pl
from jax.experimental.pallas import tpu as pltpu
from jax.sharding import PartitionSpec as P

BLOCK = 64
SPAN = 256
VCAP = 2
GROUP = 12
BUNDLE = 4
LOWEST = -1e30
MESH = pl.DeviceIdType.MESH
VMEM_LIMIT = 56 * 1024 * 1024


def lane_fold(x, op):
    parts = [x[:, i * 128 : (i + 1) * 128] for i in range(x.shape[1] // 128)]
    return functools.reduce(op, parts)


def to_row(column):
    return jnp.transpose(jnp.broadcast_to(column, (column.shape[0], 128)))[0:1, :]


def slash_kernel(
    factor, heads, length, list_ref, count_ref, q_ref, k_ref, v_ref, o_ref, lse_ref, s_ref
):
    kv = pl.program_id(0)
    owners = q_ref.shape[0]
    width = GROUP * BLOCK
    bundle = min(BUNDLE, heads)
    chains = [(a, i) for a in range(bundle) for i in range(2)]

    def one_bundle(it, carry):
        first_head = (it // owners) * bundle
        c = lax.rem(it, owners)
        hh = [first_head + a for a, _ in chains]
        block = [2 * c + i for _, i in chains]
        pair = [(kv * heads + h) * (2 * owners) + b for h, b in zip(hh, block)]
        counts = [count_ref[p] for p in pair]
        most = functools.reduce(jnp.maximum, counts)
        groups = lax.div(most + (GROUP - 1), GROUP)

        def gathered(ref, n, t):
            at = pair[n] * length + t * GROUP
            rows = [
                ref[0, pl.ds(pl.multiple_of(list_ref[at + g], BLOCK), BLOCK), :] for g in range(GROUP)
            ]
            return jnp.concatenate(rows, axis=0)

        def first(t, best):
            new = []
            for n, (_, i) in enumerate(chains):
                s = lax.dot_general(
                    q_ref[c, hh[n], i * BLOCK : (i + 1) * BLOCK, :],
                    gathered(k_ref, n, t),
                    (((1,), (1,)), ((), ())),
                    preferred_element_type=jnp.float32,
                )
                s_ref[n, t] = s
                new.append(jnp.maximum(best[n], lane_fold(s, jnp.maximum)))
            return tuple(new)

        low = jnp.full((BLOCK, 128), LOWEST, jnp.float32)
        best = lax.fori_loop(0, groups, first, (low,) * len(chains))

        key = lax.broadcasted_iota(jnp.int32, (BLOCK, width), 1)
        for n in range(len(chains)):

            def hide(t, carry, n=n):
                s_ref[n, t] = jnp.where(key < (counts[n] - t * GROUP) * BLOCK, s_ref[n, t], LOWEST)
                return carry

            lax.fori_loop(lax.div(counts[n], GROUP), groups, hide, 0)

        top = [jnp.max(b, axis=1, keepdims=True) for b in best]

        def second(t, state):
            new = []
            for n in range(len(chains)):
                total, acc = state[n]
                p = jnp.exp2((s_ref[n, t] - top[n]) * factor)
                total = total + lane_fold(p, jnp.add)
                acc = acc + jnp.dot(
                    p.astype(jnp.bfloat16), gathered(v_ref, n, t), preferred_element_type=jnp.float32
                )
                new.append((total, acc))
            return tuple(new)

        zero = jnp.zeros((BLOCK, 128), jnp.float32)
        state = lax.fori_loop(0, groups, second, ((zero, zero),) * len(chains))
        lse = []
        for n, (_, i) in enumerate(chains):
            total = jnp.sum(state[n][0], axis=1, keepdims=True)
            some = total > 0.0
            safe = jnp.where(some, total, 1.0)
            part = (state[n][1] / safe).astype(o_ref.dtype)
            o_ref[c, hh[n], i * BLOCK : (i + 1) * BLOCK, :] = part
            lse.append(jnp.where(some, top[n] * factor + jnp.log2(safe), LOWEST))
        for a in range(bundle):
            row = to_row(jnp.concatenate(lse[2 * a : 2 * a + 2], axis=0))
            lse_ref[c, 0, pl.ds(first_head + a, 1), :] = row
        return carry

    lax.fori_loop(0, heads // bundle * owners, one_bundle, 0)


def slash_attention(lists, counts, queries, keys, values, factor):
    owners, head_count, rows, hd = queries.shape
    kv_heads, key_rows, _ = keys.shape
    heads = head_count // kv_heads
    length = lists.shape[-1]
    most = length // GROUP
    elements = head_count * rows * owners * 48 * BLOCK
    return pl.pallas_call(
        functools.partial(slash_kernel, factor, heads, length),
        grid_spec=pltpu.PrefetchScalarGridSpec(
            num_scalar_prefetch=2,
            grid=(kv_heads,),
            in_specs=[
                pl.BlockSpec((owners, heads, rows, hd), lambda g, *_: (0, g, 0, 0)),
                pl.BlockSpec((1, key_rows, hd), lambda g, *_: (g, 0, 0)),
                pl.BlockSpec((1, key_rows, hd), lambda g, *_: (g, 0, 0)),
            ],
            out_specs=[
                pl.BlockSpec((owners, heads, rows, hd), lambda g, *_: (0, g, 0, 0)),
                pl.BlockSpec((owners, 1, heads, rows), lambda g, *_: (0, g, 0, 0)),
            ],
            scratch_shapes=[pltpu.VMEM((2 * min(BUNDLE, heads), most, BLOCK, GROUP * BLOCK), jnp.float32)],
        ),
        out_shape=[
            jax.ShapeDtypeStruct(queries.shape, jnp.bfloat16),
            jax.ShapeDtypeStruct((owners, kv_heads, heads, rows), jnp.float32),
        ],
        compiler_params=pltpu.CompilerParams(vmem_limit_bytes=VMEM_LIMIT),
        cost_estimate=pl.CostEstimate(
            flops=4 * elements * hd, bytes_accessed=12 * 2**20, transcendentals=elements
        ),
    )(lists.reshape(-1), counts.reshape(-1), queries, keys, values)


def local_head(factor, q_ref, kv_ref, vv_ref, kn_ref, vn_ref, bias_ref, o_ref, lse_ref):
    rows, hd = q_ref.shape[1:]
    blocks = rows // BLOCK

    def flat(ref):
        return ref[...].reshape(-1, hd)

    def scores(keys, kind):
        s = lax.dot_general(
            q_ref[0], keys, (((1,), (1,)), ((), ())), preferred_element_type=jnp.float32
        )
        bias = bias_ref[0, kind]
        parts = [s[i * BLOCK : (i + 1) * BLOCK] + bias[i : i + 1] for i in range(blocks)]
        return jnp.concatenate(parts, axis=0)

    s_vert = scores(flat(kv_ref), 0)
    s_new = scores(flat(kn_ref), 1)
    key = lax.broadcasted_iota(jnp.int32, s_new.shape, 1)
    row = lax.broadcasted_iota(jnp.int32, s_new.shape, 0) + lax.axis_index("ctx") * rows
    s_new = jnp.where(key <= row, s_new, LOWEST)
    top = jnp.maximum(
        jnp.max(lane_fold(s_vert, jnp.maximum), axis=1, keepdims=True),
        jnp.max(lane_fold(s_new, jnp.maximum), axis=1, keepdims=True),
    )
    p_vert = jnp.exp2((s_vert - top) * factor)
    p_new = jnp.exp2((s_new - top) * factor)
    total = jnp.sum(lane_fold(p_vert, jnp.add) + lane_fold(p_new, jnp.add), axis=1, keepdims=True)
    acc = jnp.dot(
        p_vert.astype(jnp.bfloat16), flat(vv_ref), preferred_element_type=jnp.float32
    ) + jnp.dot(p_new.astype(jnp.bfloat16), flat(vn_ref), preferred_element_type=jnp.float32)
    o_ref[0] = acc / total
    lse_ref[0] = to_row(top * factor + jnp.log2(total))


def local_kernel(
    factor, holders, q_ref, kv_ref, vv_ref, kn_ref, vn_ref, bias_ref, o_ref, l_ref,
    own_ref, own_lse_ref, part_ref, plse_ref, o_send, l_send, o_recv, l_recv, o_own, l_own,
):
    size = lax.axis_size("ctx")
    me = lax.axis_index("ctx")
    kvh = lax.axis_index("kvh")
    first = size - holders
    turn = pl.program_id(0)
    last = pl.num_programs(0) - 1

    def copies(r, step):
        to = lax.rem(me + step, size)
        pairs = ((o_ref, part_ref, o_send, o_recv), (l_ref, plse_ref, l_send, l_recv))
        return [
            pltpu.make_async_remote_copy(
                src_ref=src.at[to],
                dst_ref=dst.at[r],
                send_sem=send.at[step - 1],
                recv_sem=recv.at[r],
                device_id=(to, kvh),
                device_id_type=MESH,
            )
            for src, dst, send, recv in pairs
        ]

    def own_copies(r):
        return [
            pltpu.make_async_copy(o_ref.at[me], part_ref.at[r], o_own),
            pltpu.make_async_copy(l_ref.at[me], plse_ref.at[r], l_own),
        ]

    @pl.when(turn == 0)
    def _():
        barrier = pltpu.get_barrier_semaphore()
        for r in range(holders):

            @pl.when(me != first + r)
            def _():
                pl.semaphore_signal(barrier, inc=1, device_id=(first + r, kvh), device_id_type=MESH)

        for r in range(holders):

            @pl.when(me == first + r)
            def _():
                pl.semaphore_wait(barrier, size - 1)
                for step in range(1, size):
                    for copy in copies(r, step):
                        copy.start()
                for copy in own_copies(r):
                    copy.start()

    local_head(factor, q_ref, kv_ref, vv_ref, kn_ref, vn_ref, bias_ref, own_ref, own_lse_ref)

    @pl.when(turn == last)
    def _():
        for r in range(holders):

            @pl.when(me == first + r)
            def _():
                for copy in own_copies(r):
                    copy.wait()
                for step in range(1, size):
                    for copy in copies(r, step):
                        copy.wait_send()

            @pl.when(me != first + r)
            def _():
                for copy in copies(r, 1):
                    copy.wait_recv()


def local_attention(queries, gathered, bias, kv_heads, factor, slash_o, slash_lse, holders):
    head_count, rows, hd = queries.shape
    owners = gathered.shape[0]
    blocks = rows // BLOCK
    group = head_count // kv_heads
    piece = (owners, 2, BLOCK, hd)
    return pl.pallas_call(
        functools.partial(local_kernel, factor, holders),
        grid=(head_count,),
        in_specs=[
            pl.BlockSpec((1, rows, hd), lambda h: (h, 0, 0)),
            pl.BlockSpec(piece, lambda h: (0, h, 0, 0)),
            pl.BlockSpec(piece, lambda h: (0, head_count + h, 0, 0)),
            pl.BlockSpec(piece, lambda h: (0, 2 * head_count + h // group, 0, 0)),
            pl.BlockSpec(piece, lambda h: (0, 2 * head_count + kv_heads + h // group, 0, 0)),
            pl.BlockSpec((1, 2, blocks, bias.shape[-1]), lambda h: (h, 0, 0, 0)),
            pl.BlockSpec(memory_space=pl.ANY),
            pl.BlockSpec(memory_space=pl.ANY),
        ],
        out_specs=[
            pl.BlockSpec((1, rows, hd), lambda h: (h, 0, 0)),
            pl.BlockSpec((1, 1, rows), lambda h: (h, 0, 0)),
            pl.BlockSpec(memory_space=pl.ANY),
            pl.BlockSpec(memory_space=pl.ANY),
        ],
        out_shape=[
            jax.ShapeDtypeStruct(queries.shape, jnp.float32),
            jax.ShapeDtypeStruct((head_count, 1, rows), jnp.float32),
            jax.ShapeDtypeStruct((holders,) + slash_o.shape[1:], slash_o.dtype),
            jax.ShapeDtypeStruct((holders,) + slash_lse.shape[1:], slash_lse.dtype),
        ],
        scratch_shapes=[
            pltpu.SemaphoreType.DMA((owners - 1,)),
            pltpu.SemaphoreType.DMA((owners - 1,)),
            pltpu.SemaphoreType.DMA((holders,)),
            pltpu.SemaphoreType.DMA((holders,)),
            pltpu.SemaphoreType.DMA,
            pltpu.SemaphoreType.DMA,
        ],
        compiler_params=pltpu.CompilerParams(
            collective_id=0, has_side_effects=True, vmem_limit_bytes=VMEM_LIMIT
        ),
    )(queries, gathered, gathered, gathered, gathered, bias, slash_o, slash_lse)


def spread_kernel(y_ref, got_ref, send, recv):
    size = lax.axis_size("kvh")
    me = lax.axis_index("kvh")
    ctx = lax.axis_index("ctx")
    barrier = pltpu.get_barrier_semaphore()
    for step in range(1, size):
        to = lax.rem(me + step, size)
        pl.semaphore_signal(barrier, inc=1, device_id=(ctx, to), device_id_type=MESH)
    pl.semaphore_wait(barrier, size - 1)
    copies = []
    for step in range(1, size):
        to = lax.rem(me + step, size)
        copies.append(
            pltpu.make_async_remote_copy(
                src_ref=y_ref.at[to],
                dst_ref=got_ref.at[step - 1],
                send_sem=send.at[step - 1],
                recv_sem=recv.at[step - 1],
                device_id=(ctx, to),
                device_id_type=MESH,
            )
        )
    for copy in copies:
        copy.start()
    for copy in copies:
        copy.wait()


def sum_over_kvh(y):
    size = lax.axis_size("kvh")
    y = y.reshape(size, y.shape[0] // size, y.shape[1])
    got = pl.pallas_call(
        spread_kernel,
        out_shape=jax.ShapeDtypeStruct((size - 1,) + y.shape[1:], y.dtype),
        in_specs=[pl.BlockSpec(memory_space=pl.ANY)],
        out_specs=pl.BlockSpec(memory_space=pl.ANY),
        scratch_shapes=[
            pltpu.SemaphoreType.DMA((size - 1,)),
            pltpu.SemaphoreType.DMA((size - 1,)),
        ],
        compiler_params=pltpu.CompilerParams(collective_id=1, has_side_effects=True),
    )(y)
    own = lax.dynamic_index_in_dim(y, lax.axis_index("kvh"), axis=0, keepdims=False)
    total = own.astype(jnp.float32) + jnp.sum(got.astype(jnp.float32), axis=0)
    return total.astype(y.dtype)


def block_lists(offsets, block_ids, base, blocks_dev):
    diagonals = offsets.shape[1]
    length = -(-diagonals // GROUP) * GROUP
    rank = jnp.sum((offsets[:, :, None] > offsets[:, None, :]).astype(jnp.int32), axis=2)
    found = base + block_ids[None, :, None] - offsets[:, None, :]
    inside = (found >= 0) & (found < blocks_dev)
    counts = jnp.sum(inside.astype(jnp.int32), axis=2)
    below = jnp.sum((found >= blocks_dev).astype(jnp.int32), axis=2)
    place = jnp.arange(length, dtype=jnp.int32)
    place = below[:, :, None] + jnp.minimum(place[None, None, :], counts[:, :, None] - 1)
    chosen = inside[:, :, None, :] & (rank[:, None, None, :] == place[:, :, :, None])
    lists = jnp.sum(jnp.where(chosen, found[:, :, None, :] * BLOCK, 0), axis=3)
    return lists, counts


def slots_of(verticals, lower_block, blocks_dev):
    inside = (verticals >= lower_block) & (verticals < lower_block + blocks_dev)
    counts = inside.astype(jnp.int32)
    slot_rank = jnp.cumsum(counts, axis=1) - counts
    slot_ids = jnp.arange(VCAP, dtype=jnp.int32)
    onehot = inside[:, None, :] & (slot_rank[:, None, :] == slot_ids[None, :, None])
    filled = jnp.any(onehot, axis=2)
    block = jnp.sum(jnp.where(onehot, verticals[:, None, :], 0), axis=2)
    return jnp.where(filled, block, -1)


def shards(queries, new_keys, new_values, cache_keys, cache_values, verticals, offsets, out_weight):
    own_rows, head_count, hd = queries.shape
    kv_heads = cache_keys.shape[1]
    size = lax.axis_size("ctx")
    me = lax.axis_index("ctx")
    cache_rows = cache_keys.shape[0]
    blocks_dev = cache_rows // BLOCK
    cache_blocks = blocks_dev * size
    own_blocks = own_rows // BLOCK
    holders = SPAN // blocks_dev
    group = head_count // kv_heads
    factor = math.log2(math.e) / math.sqrt(hd)

    q_own = jnp.transpose(queries, (1, 0, 2))
    q_all = lax.all_gather(q_own, "ctx", axis=0, tiled=False)

    keys = jnp.transpose(cache_keys, (1, 0, 2))
    values = jnp.transpose(cache_values, (1, 0, 2))
    mine = slots_of(verticals, me * blocks_dev, blocks_dev)
    local_block = jnp.where(mine >= 0, mine - me * blocks_dev, 0)
    kv_of = (jnp.arange(head_count, dtype=jnp.int32) // group)[:, None]
    flat_block = (kv_of * blocks_dev + local_block).reshape(-1)
    slot_keys = keys.reshape(-1, BLOCK, hd)[flat_block]
    slot_values = values.reshape(-1, BLOCK, hd)[flat_block]
    fresh_keys = jnp.transpose(new_keys, (1, 0, 2)).reshape(-1, BLOCK, hd)
    fresh_values = jnp.transpose(new_values, (1, 0, 2)).reshape(-1, BLOCK, hd)
    packed = jnp.concatenate([slot_keys, slot_values, fresh_keys, fresh_values], axis=0)
    gathered = lax.all_gather(packed, "ctx", axis=0, tiled=False)

    holder = me - (size - holders)
    block_ids = jnp.arange(size * own_blocks, dtype=jnp.int32)
    lists, counts = block_lists(offsets, block_ids, SPAN - holder * blocks_dev, blocks_dev)
    counts = jnp.where(holder >= 0, counts, 0)
    slash_o, slash_lse = slash_attention(lists, counts, q_all, keys, values, factor)

    own_ids = me * own_blocks + jnp.arange(own_blocks, dtype=jnp.int32)
    slots = jnp.stack([slots_of(verticals, c * blocks_dev, blocks_dev) for c in range(size)], axis=1)
    slots = slots.reshape(head_count, size * VCAP)
    slash_blocks = cache_blocks + own_ids[None, :, None] - offsets[:, None, :]
    repeated = jnp.any(slots[:, None, :, None] == slash_blocks[:, :, None, :], axis=-1)
    vert_ok = (slots[:, None, :] >= 0) & jnp.logical_not(repeated)
    new_ids = cache_blocks + jnp.arange(size * own_blocks, dtype=jnp.int32)
    new_ok = jnp.any(new_ids[None, None, :, None] == slash_blocks[:, :, None, :], axis=-1)
    bias = jnp.where(jnp.stack([vert_ok, new_ok], axis=1), 0.0, LOWEST).astype(jnp.float32)
    bias = jnp.repeat(bias, BLOCK, axis=-1)
    own_o, own_lse, part_o, part_lse = local_attention(
        q_own, gathered, bias, kv_heads, factor, slash_o, slash_lse, holders
    )

    own_lse = own_lse.reshape(head_count, own_rows)
    part_lse = part_lse.reshape(holders, head_count, own_rows)
    top = jnp.maximum(own_lse, jnp.max(part_lse, axis=0))
    own_share = jnp.exp2(own_lse - top)
    part_share = jnp.exp2(part_lse - top[None])
    whole = own_share + jnp.sum(part_share, axis=0)
    mixed = own_o * (own_share / whole)[..., None] + jnp.sum(
        part_o.astype(jnp.float32) * (part_share / whole[None])[..., None], axis=0
    )
    attended = jnp.transpose(mixed.astype(jnp.bfloat16), (1, 0, 2)).reshape(own_rows, head_count * hd)
    return sum_over_kvh(
        jnp.dot(attended, out_weight, preferred_element_type=jnp.float32).astype(jnp.bfloat16)
    )


def solution(mesh):
    return jax.shard_map(
        shards,
        mesh=mesh,
        in_specs=(
            P("ctx", "kvh", None),
            P("ctx", "kvh", None),
            P("ctx", "kvh", None),
            P("ctx", "kvh", None),
            P("ctx", "kvh", None),
            P("kvh", None),
            P("kvh", None),
            P("kvh", None),
        ),
        out_specs=P(("ctx", "kvh"), None),
        check_vma=False,
    )
```

```python
import functools
import math

import jax
import jax.numpy as jnp
from jax import lax
from jax.experimental import pallas as pl
from jax.experimental.pallas import tpu as pltpu
from jax.sharding import PartitionSpec as P

BLOCK = 64
SPAN = 256
VCAP = 2
GROUP = 12
BUNDLE = 4
LOWEST = -1e30
MESH = pl.DeviceIdType.MESH
VMEM_LIMIT = 56 * 1024 * 1024


def lane_fold(x, op):
    parts = [x[:, i * 128 : (i + 1) * 128] for i in range(x.shape[1] // 128)]
    return functools.reduce(op, parts)


def to_row(column):
    return jnp.transpose(jnp.broadcast_to(column, (column.shape[0], 128)))[0:1, :]


def slash_kernel(
    factor, heads, length, list_ref, count_ref, q_ref, k_ref, v_ref, o_ref, lse_ref, s_ref
):
    kv = pl.program_id(0)
    owners = q_ref.shape[0]
    width = GROUP * BLOCK
    bundle = min(BUNDLE, heads)
    chains = [(a, i) for a in range(bundle) for i in range(2)]

    def one_bundle(it, carry):
        first_head = (it // owners) * bundle
        c = lax.rem(it, owners)
        hh = [first_head + a for a, _ in chains]
        block = [2 * c + i for _, i in chains]
        pair = [(kv * heads + h) * (2 * owners) + b for h, b in zip(hh, block)]
        counts = [count_ref[p] for p in pair]
        most = functools.reduce(jnp.maximum, counts)
        groups = lax.div(most + (GROUP - 1), GROUP)

        def gathered(ref, n, t):
            at = pair[n] * length + t * GROUP
            rows = [
                ref[0, pl.ds(pl.multiple_of(list_ref[at + g], BLOCK), BLOCK), :] for g in range(GROUP)
            ]
            return jnp.concatenate(rows, axis=0)

        def first(t, best):
            new = []
            for n, (_, i) in enumerate(chains):
                s = lax.dot_general(
                    q_ref[c, hh[n], i * BLOCK : (i + 1) * BLOCK, :],
                    gathered(k_ref, n, t),
                    (((1,), (1,)), ((), ())),
                    preferred_element_type=jnp.float32,
                )
                s_ref[n, t] = s
                new.append(jnp.maximum(best[n], lane_fold(s, jnp.maximum)))
            return tuple(new)

        low = jnp.full((BLOCK, 128), LOWEST, jnp.float32)
        best = lax.fori_loop(0, groups, first, (low,) * len(chains))

        key = lax.broadcasted_iota(jnp.int32, (BLOCK, width), 1)
        for n in range(len(chains)):

            def hide(t, carry, n=n):
                s_ref[n, t] = jnp.where(key < (counts[n] - t * GROUP) * BLOCK, s_ref[n, t], LOWEST)
                return carry

            lax.fori_loop(lax.div(counts[n], GROUP), groups, hide, 0)

        top = [jnp.max(b, axis=1, keepdims=True) for b in best]

        def second(t, state):
            new = []
            for n in range(len(chains)):
                total, acc = state[n]
                p = jnp.exp2((s_ref[n, t] - top[n]) * factor)
                total = total + lane_fold(p, jnp.add)
                acc = acc + jnp.dot(
                    p.astype(jnp.bfloat16), gathered(v_ref, n, t), preferred_element_type=jnp.float32
                )
                new.append((total, acc))
            return tuple(new)

        zero = jnp.zeros((BLOCK, 128), jnp.float32)
        state = lax.fori_loop(0, groups, second, ((zero, zero),) * len(chains))
        lse = []
        for n, (_, i) in enumerate(chains):
            total = jnp.sum(state[n][0], axis=1, keepdims=True)
            some = total > 0.0
            safe = jnp.where(some, total, 1.0)
            part = (state[n][1] / safe).astype(o_ref.dtype)
            o_ref[c, hh[n], i * BLOCK : (i + 1) * BLOCK, :] = part
            lse.append(jnp.where(some, top[n] * factor + jnp.log2(safe), LOWEST))
        for a in range(bundle):
            row = to_row(jnp.concatenate(lse[2 * a : 2 * a + 2], axis=0))
            lse_ref[c, 0, pl.ds(first_head + a, 1), :] = row
        return carry

    lax.fori_loop(0, heads // bundle * owners, one_bundle, 0)


def slash_attention(lists, counts, queries, keys, values, factor):
    owners, head_count, rows, hd = queries.shape
    kv_heads, key_rows, _ = keys.shape
    heads = head_count // kv_heads
    length = lists.shape[-1]
    most = length // GROUP
    elements = head_count * rows * owners * 48 * BLOCK
    return pl.pallas_call(
        functools.partial(slash_kernel, factor, heads, length),
        grid_spec=pltpu.PrefetchScalarGridSpec(
            num_scalar_prefetch=2,
            grid=(kv_heads,),
            in_specs=[
                pl.BlockSpec((owners, heads, rows, hd), lambda g, *_: (0, g, 0, 0)),
                pl.BlockSpec((1, key_rows, hd), lambda g, *_: (g, 0, 0)),
                pl.BlockSpec((1, key_rows, hd), lambda g, *_: (g, 0, 0)),
            ],
            out_specs=[
                pl.BlockSpec((owners, heads, rows, hd), lambda g, *_: (0, g, 0, 0)),
                pl.BlockSpec((owners, 1, heads, rows), lambda g, *_: (0, g, 0, 0)),
            ],
            scratch_shapes=[pltpu.VMEM((2 * min(BUNDLE, heads), most, BLOCK, GROUP * BLOCK), jnp.float32)],
        ),
        out_shape=[
            jax.ShapeDtypeStruct(queries.shape, jnp.bfloat16),
            jax.ShapeDtypeStruct((owners, kv_heads, heads, rows), jnp.float32),
        ],
        compiler_params=pltpu.CompilerParams(vmem_limit_bytes=VMEM_LIMIT),
        cost_estimate=pl.CostEstimate(
            flops=4 * elements * hd, bytes_accessed=12 * 2**20, transcendentals=elements
        ),
    )(lists.reshape(-1), counts.reshape(-1), queries, keys, values)


def local_head(factor, q_ref, kv_ref, vv_ref, kn_ref, vn_ref, bias_ref, o_ref, lse_ref):
    rows, hd = q_ref.shape[1:]
    blocks = rows // BLOCK

    def flat(ref):
        return ref[...].reshape(-1, hd)

    def scores(keys, kind):
        s = lax.dot_general(
            q_ref[0], keys, (((1,), (1,)), ((), ())), preferred_element_type=jnp.float32
        )
        bias = bias_ref[0, kind]
        parts = [s[i * BLOCK : (i + 1) * BLOCK] + bias[i : i + 1] for i in range(blocks)]
        return jnp.concatenate(parts, axis=0)

    s_vert = scores(flat(kv_ref), 0)
    s_new = scores(flat(kn_ref), 1)
    key = lax.broadcasted_iota(jnp.int32, s_new.shape, 1)
    row = lax.broadcasted_iota(jnp.int32, s_new.shape, 0) + lax.axis_index("ctx") * rows
    s_new = jnp.where(key <= row, s_new, LOWEST)
    top = jnp.maximum(
        jnp.max(lane_fold(s_vert, jnp.maximum), axis=1, keepdims=True),
        jnp.max(lane_fold(s_new, jnp.maximum), axis=1, keepdims=True),
    )
    p_vert = jnp.exp2((s_vert - top) * factor)
    p_new = jnp.exp2((s_new - top) * factor)
    total = jnp.sum(lane_fold(p_vert, jnp.add) + lane_fold(p_new, jnp.add), axis=1, keepdims=True)
    acc = jnp.dot(
        p_vert.astype(jnp.bfloat16), flat(vv_ref), preferred_element_type=jnp.float32
    ) + jnp.dot(p_new.astype(jnp.bfloat16), flat(vn_ref), preferred_element_type=jnp.float32)
    o_ref[0] = acc / total
    lse_ref[0] = to_row(top * factor + jnp.log2(total))


def local_kernel(
    factor, holders, q_ref, kv_ref, vv_ref, kn_ref, vn_ref, bias_ref, o_ref, l_ref,
    own_ref, own_lse_ref, part_ref, plse_ref, o_send, l_send, o_recv, l_recv, o_own, l_own,
):
    size = lax.axis_size("ctx")
    me = lax.axis_index("ctx")
    kvh = lax.axis_index("kvh")
    first = size - holders
    turn = pl.program_id(0)
    last = pl.num_programs(0) - 1

    def copies(r, step):
        to = lax.rem(me + step, size)
        pairs = ((o_ref, part_ref, o_send, o_recv), (l_ref, plse_ref, l_send, l_recv))
        return [
            pltpu.make_async_remote_copy(
                src_ref=src.at[to],
                dst_ref=dst.at[r],
                send_sem=send.at[step - 1],
                recv_sem=recv.at[r],
                device_id=(to, kvh),
                device_id_type=MESH,
            )
            for src, dst, send, recv in pairs
        ]

    def own_copies(r):
        return [
            pltpu.make_async_copy(o_ref.at[me], part_ref.at[r], o_own),
            pltpu.make_async_copy(l_ref.at[me], plse_ref.at[r], l_own),
        ]

    @pl.when(turn == 0)
    def _():
        barrier = pltpu.get_barrier_semaphore()
        for r in range(holders):

            @pl.when(me != first + r)
            def _():
                pl.semaphore_signal(barrier, inc=1, device_id=(first + r, kvh), device_id_type=MESH)

        for r in range(holders):

            @pl.when(me == first + r)
            def _():
                pl.semaphore_wait(barrier, size - 1)
                for step in range(1, size):
                    for copy in copies(r, step):
                        copy.start()
                for copy in own_copies(r):
                    copy.start()

    local_head(factor, q_ref, kv_ref, vv_ref, kn_ref, vn_ref, bias_ref, own_ref, own_lse_ref)

    @pl.when(turn == last)
    def _():
        for r in range(holders):

            @pl.when(me == first + r)
            def _():
                for copy in own_copies(r):
                    copy.wait()
                for step in range(1, size):
                    for copy in copies(r, step):
                        copy.wait_send()

            @pl.when(me != first + r)
            def _():
                for copy in copies(r, 1):
                    copy.wait_recv()


def local_attention(queries, gathered, bias, kv_heads, factor, slash_o, slash_lse, holders):
    head_count, rows, hd = queries.shape
    owners = gathered.shape[0]
    blocks = rows // BLOCK
    group = head_count // kv_heads
    piece = (owners, 2, BLOCK, hd)
    return pl.pallas_call(
        functools.partial(local_kernel, factor, holders),
        grid=(head_count,),
        in_specs=[
            pl.BlockSpec((1, rows, hd), lambda h: (h, 0, 0)),
            pl.BlockSpec(piece, lambda h: (0, h, 0, 0)),
            pl.BlockSpec(piece, lambda h: (0, head_count + h, 0, 0)),
            pl.BlockSpec(piece, lambda h: (0, 2 * head_count + h // group, 0, 0)),
            pl.BlockSpec(piece, lambda h: (0, 2 * head_count + kv_heads + h // group, 0, 0)),
            pl.BlockSpec((1, 2, blocks, bias.shape[-1]), lambda h: (h, 0, 0, 0)),
            pl.BlockSpec(memory_space=pl.ANY),
            pl.BlockSpec(memory_space=pl.ANY),
        ],
        out_specs=[
            pl.BlockSpec((1, rows, hd), lambda h: (h, 0, 0)),
            pl.BlockSpec((1, 1, rows), lambda h: (h, 0, 0)),
            pl.BlockSpec(memory_space=pl.ANY),
            pl.BlockSpec(memory_space=pl.ANY),
        ],
        out_shape=[
            jax.ShapeDtypeStruct(queries.shape, jnp.float32),
            jax.ShapeDtypeStruct((head_count, 1, rows), jnp.float32),
            jax.ShapeDtypeStruct((holders,) + slash_o.shape[1:], slash_o.dtype),
            jax.ShapeDtypeStruct((holders,) + slash_lse.shape[1:], slash_lse.dtype),
        ],
        scratch_shapes=[
            pltpu.SemaphoreType.DMA((owners - 1,)),
            pltpu.SemaphoreType.DMA((owners - 1,)),
            pltpu.SemaphoreType.DMA((holders,)),
            pltpu.SemaphoreType.DMA((holders,)),
            pltpu.SemaphoreType.DMA,
            pltpu.SemaphoreType.DMA,
        ],
        compiler_params=pltpu.CompilerParams(
            collective_id=0, has_side_effects=True, vmem_limit_bytes=VMEM_LIMIT
        ),
    )(queries, gathered, gathered, gathered, gathered, bias, slash_o, slash_lse)


def spread_kernel(y_ref, got_ref, send, recv):
    size = lax.axis_size("kvh")
    me = lax.axis_index("kvh")
    ctx = lax.axis_index("ctx")
    barrier = pltpu.get_barrier_semaphore()
    for step in range(1, size):
        to = lax.rem(me + step, size)
        pl.semaphore_signal(barrier, inc=1, device_id=(ctx, to), device_id_type=MESH)
    pl.semaphore_wait(barrier, size - 1)
    copies = []
    for step in range(1, size):
        to = lax.rem(me + step, size)
        copies.append(
            pltpu.make_async_remote_copy(
                src_ref=y_ref.at[to],
                dst_ref=got_ref.at[step - 1],
                send_sem=send.at[step - 1],
                recv_sem=recv.at[step - 1],
                device_id=(ctx, to),
                device_id_type=MESH,
            )
        )
    for copy in copies:
        copy.start()
    for copy in copies:
        copy.wait()


def sum_over_kvh(y):
    size = lax.axis_size("kvh")
    y = y.reshape(size, y.shape[0] // size, y.shape[1])
    got = pl.pallas_call(
        spread_kernel,
        out_shape=jax.ShapeDtypeStruct((size - 1,) + y.shape[1:], y.dtype),
        in_specs=[pl.BlockSpec(memory_space=pl.ANY)],
        out_specs=pl.BlockSpec(memory_space=pl.ANY),
        scratch_shapes=[
            pltpu.SemaphoreType.DMA((size - 1,)),
            pltpu.SemaphoreType.DMA((size - 1,)),
        ],
        compiler_params=pltpu.CompilerParams(collective_id=1, has_side_effects=True),
    )(y)
    own = lax.dynamic_index_in_dim(y, lax.axis_index("kvh"), axis=0, keepdims=False)
    total = own.astype(jnp.float32) + jnp.sum(got.astype(jnp.float32), axis=0)
    return total.astype(y.dtype)


def block_lists(offsets, block_ids, base, blocks_dev):
    diagonals = offsets.shape[1]
    length = -(-diagonals // GROUP) * GROUP
    rank = jnp.sum((offsets[:, :, None] > offsets[:, None, :]).astype(jnp.int32), axis=2)
    found = base + block_ids[None, :, None] - offsets[:, None, :]
    inside = (found >= 0) & (found < blocks_dev)
    counts = jnp.sum(inside.astype(jnp.int32), axis=2)
    below = jnp.sum((found >= blocks_dev).astype(jnp.int32), axis=2)
    place = jnp.arange(length, dtype=jnp.int32)
    place = below[:, :, None] + jnp.minimum(place[None, None, :], counts[:, :, None] - 1)
    chosen = inside[:, :, None, :] & (rank[:, None, None, :] == place[:, :, :, None])
    lists = jnp.sum(jnp.where(chosen, found[:, :, None, :] * BLOCK, 0), axis=3)
    return lists, counts


def slots_of(verticals, lower_block, blocks_dev):
    inside = (verticals >= lower_block) & (verticals < lower_block + blocks_dev)
    counts = inside.astype(jnp.int32)
    slot_rank = jnp.cumsum(counts, axis=1) - counts
    slot_ids = jnp.arange(VCAP, dtype=jnp.int32)
    onehot = inside[:, None, :] & (slot_rank[:, None, :] == slot_ids[None, :, None])
    filled = jnp.any(onehot, axis=2)
    block = jnp.sum(jnp.where(onehot, verticals[:, None, :], 0), axis=2)
    return jnp.where(filled, block, -1)


def shards(queries, new_keys, new_values, cache_keys, cache_values, verticals, offsets, out_weight):
    own_rows, head_count, hd = queries.shape
    kv_heads = cache_keys.shape[1]
    size = lax.axis_size("ctx")
    me = lax.axis_index("ctx")
    cache_rows = cache_keys.shape[0]
    blocks_dev = cache_rows // BLOCK
    cache_blocks = blocks_dev * size
    own_blocks = own_rows // BLOCK
    holders = SPAN // blocks_dev
    group = head_count // kv_heads
    factor = math.log2(math.e) / math.sqrt(hd)

    q_own = jnp.transpose(queries, (1, 0, 2))
    q_all = [
        lax.all_gather(q_own[g * group : (g + 1) * group], "ctx", axis=0, tiled=False)
        for g in range(kv_heads)
    ]

    keys = jnp.transpose(cache_keys, (1, 0, 2))
    values = jnp.transpose(cache_values, (1, 0, 2))
    mine = slots_of(verticals, me * blocks_dev, blocks_dev)
    local_block = jnp.where(mine >= 0, mine - me * blocks_dev, 0)
    kv_of = (jnp.arange(head_count, dtype=jnp.int32) // group)[:, None]
    flat_block = (kv_of * blocks_dev + local_block).reshape(-1)
    slot_keys = keys.reshape(-1, BLOCK, hd)[flat_block]
    slot_values = values.reshape(-1, BLOCK, hd)[flat_block]
    fresh_keys = jnp.transpose(new_keys, (1, 0, 2)).reshape(-1, BLOCK, hd)
    fresh_values = jnp.transpose(new_values, (1, 0, 2)).reshape(-1, BLOCK, hd)
    packed = jnp.concatenate([slot_keys, slot_values, fresh_keys, fresh_values], axis=0)
    gathered = lax.all_gather(packed, "ctx", axis=0, tiled=False)

    holder = me - (size - holders)
    block_ids = jnp.arange(size * own_blocks, dtype=jnp.int32)
    lists, counts = block_lists(offsets, block_ids, SPAN - holder * blocks_dev, blocks_dev)
    counts = jnp.where(holder >= 0, counts, 0)
    parts = [
        slash_attention(
            lists[g * group : (g + 1) * group],
            counts[g * group : (g + 1) * group],
            q_all[g],
            keys[g : g + 1],
            values[g : g + 1],
            factor,
        )
        for g in range(kv_heads)
    ]
    slash_o = jnp.concatenate([o for o, _ in parts], axis=1)
    slash_lse = jnp.concatenate([lse for _, lse in parts], axis=1)

    own_ids = me * own_blocks + jnp.arange(own_blocks, dtype=jnp.int32)
    slots = jnp.stack([slots_of(verticals, c * blocks_dev, blocks_dev) for c in range(size)], axis=1)
    slots = slots.reshape(head_count, size * VCAP)
    slash_blocks = cache_blocks + own_ids[None, :, None] - offsets[:, None, :]
    repeated = jnp.any(slots[:, None, :, None] == slash_blocks[:, :, None, :], axis=-1)
    vert_ok = (slots[:, None, :] >= 0) & jnp.logical_not(repeated)
    new_ids = cache_blocks + jnp.arange(size * own_blocks, dtype=jnp.int32)
    new_ok = jnp.any(new_ids[None, None, :, None] == slash_blocks[:, :, None, :], axis=-1)
    bias = jnp.where(jnp.stack([vert_ok, new_ok], axis=1), 0.0, LOWEST).astype(jnp.float32)
    bias = jnp.repeat(bias, BLOCK, axis=-1)
    own_o, own_lse, part_o, part_lse = local_attention(
        q_own, gathered, bias, kv_heads, factor, slash_o, slash_lse, holders
    )

    own_lse = own_lse.reshape(head_count, own_rows)
    part_lse = part_lse.reshape(holders, head_count, own_rows)
    top = jnp.maximum(own_lse, jnp.max(part_lse, axis=0))
    own_share = jnp.exp2(own_lse - top)
    part_share = jnp.exp2(part_lse - top[None])
    whole = own_share + jnp.sum(part_share, axis=0)
    mixed = own_o * (own_share / whole)[..., None] + jnp.sum(
        part_o.astype(jnp.float32) * (part_share / whole[None])[..., None], axis=0
    )
    attended = jnp.transpose(mixed.astype(jnp.bfloat16), (1, 0, 2)).reshape(own_rows, head_count * hd)
    return sum_over_kvh(
        jnp.dot(attended, out_weight, preferred_element_type=jnp.float32).astype(jnp.bfloat16)
    )


def solution(mesh):
    return jax.shard_map(
        shards,
        mesh=mesh,
        in_specs=(
            P("ctx", "kvh", None),
            P("ctx", "kvh", None),
            P("ctx", "kvh", None),
            P("ctx", "kvh", None),
            P("ctx", "kvh", None),
            P("kvh", None),
            P("kvh", None),
            P("kvh", None),
        ),
        out_specs=P(("ctx", "kvh"), None),
        check_vma=False,
    )
```
